128 devices in a mesh: dp: 16 (over z, x_hi, core), tensor: 8 (over y, x_lo).
Axes of the slice: x: 4 (x_hi: 2, x_lo: 2; x = x_hi * 2 + x_lo), y: 4, z: 4, core: 2. Of those that a mesh axis runs over, the one named last changes fastest.
Arguments:
- layer_input: bfloat16 [4096, 4096], P(('dp', 'tensor')), may hold values from -24 to 24
- output_grad: bfloat16 [4096, 4096], P(('dp', 'tensor')), may hold values from -24 to 24
- gate_weight: bfloat16 [4096, 7168], P(None, 'tensor'), may hold values from -0.09375 to 0.09375
- up_weight: bfloat16 [4096, 7168], P(None, 'tensor'), may hold values from -0.09375 to 0.09375
- down_weight: bfloat16 [7168, 4096], P('tensor'), may hold values from -0.0625 to 0.0625
Outputs:
- input_grad: bfloat16 [4096, 4096], P(('dp', 'tensor'))
- gate_grad: bfloat16 [4096, 7168], P('dp', 'tensor')
- up_grad: bfloat16 [4096, 7168], P('dp', 'tensor')
- down_grad: bfloat16 [7168, 4096], P('tensor', 'dp')
The draws below stay inside these ranges and needn't reach their ends.
All inputs are finite; a program needn't handle non-finite values.
Results may differ from the reference program's by a relative error of at most 0.019.
Values may be sent and summed in bfloat16 or wider, within the bound.
A program may use at most 192 MiB of HBM per device.

```python
import jax
import jax.numpy as jnp
from jax import lax

D = 4096
TOK_DEV = 256
FF = 7168
TOKENS = 4096
N_DP = 16


def with_spikes(drawn, stream_key, source, target, blocks, factor):
    def block_of(dim):
        return (jnp.arange(drawn.shape[dim]) // (drawn.shape[dim] // blocks)).reshape((-1,) + (1,) * (drawn.ndim - 1 - dim))

    near = jax.random.permutation(stream_key, blocks)[block_of(target)]
    second = (block_of(target) + blocks // 2) % blocks
    return jnp.where((block_of(source) == near) | (block_of(source) == second), factor * drawn, drawn)


def steps_of(own_key, dims, shards, least, high):
    factor_of = 1.0
    for axis_at, parts in shards:
        draws = jax.random.uniform(jax.random.fold_in(jax.random.fold_in(own_key, 6), axis_at), (parts,), jnp.float32, least / len(shards), high / len(shards))
        factor_of = factor_of * jnp.repeat(jnp.exp(draws), dims[axis_at] // parts).reshape((-1,) + (1,) * (len(dims) - 1 - axis_at))
    return factor_of


def centred(stream_key, extent, spread, most, cuts=(), held_as=jnp.bfloat16):
    result = spread * jax.random.normal(stream_key, extent, jnp.float32)
    if cuts:
        result = result * steps_of(stream_key, extent, cuts, -0.22, 0.18)
    return jnp.clip(result, -most, most).astype(held_as)


def bell_draw_with(rng, extent, deviation, most, split, heavy, kind=jnp.bfloat16):
    result = deviation * jax.random.normal(rng, extent, jnp.float32)
    if split:
        result = result * steps_of(rng, extent, split, -0.22, 0.18)
    return jnp.clip(with_spikes(result, jax.random.fold_in(rng, 3), *heavy), -most, most).astype(kind)


def setup_inputs(seed: int = 0) -> dict:
    key_list = jax.random.split(jax.random.key(seed), 6)
    layer_input = bell_draw_with(key_list[0], (TOKENS, D), 1.0, 24.0, ((0, 128),), (0, 1, 128, 5.5))
    output_grad = bell_draw_with(key_list[1], (TOKENS, D), 1.0, 24.0, ((0, 128),), (0, 1, 128, 5.5))
    gate_weight = centred(key_list[2], (D, FF), D ** -0.5, 0.09375, ((1, 8),))
    up_weight = centred(key_list[3], (D, FF), D ** -0.5, 0.09375, ((1, 8),))
    down_weight = centred(key_list[4], (FF, D), FF ** -0.5, 0.0625, ((0, 8),))
    return dict(layer_input=layer_input, output_grad=output_grad, gate_weight=gate_weight, up_weight=up_weight, down_weight=down_weight)


def times_transposed(left, right):
    return lax.dot_general(left, right, (((1,), (1,)), ((), ())), preferred_element_type=jnp.float32)


def transposed_times(left, right):
    return lax.dot_general(left, right, (((0,), (0,)), ((), ())), preferred_element_type=jnp.float32)


def reference(layer_input, output_grad, gate_weight, up_weight, down_weight):
    gate_pre = jnp.dot(layer_input, gate_weight, preferred_element_type=jnp.float32)
    up_pre = jnp.dot(layer_input, up_weight, preferred_element_type=jnp.float32)
    sigma = jax.nn.sigmoid(gate_pre)
    swish = gate_pre * sigma
    hidden = (swish * up_pre).astype(jnp.bfloat16)
    hidden_grad = times_transposed(output_grad, down_weight)
    gate_delta = (hidden_grad * up_pre * sigma * (1.0 + gate_pre * (1.0 - sigma))).astype(jnp.bfloat16)
    up_delta = (hidden_grad * swish).astype(jnp.bfloat16)
    input_grad = (times_transposed(gate_delta, gate_weight) + times_transposed(up_delta, up_weight)).astype(jnp.bfloat16)

    def group_step(totals, index):
        offset = (index * TOK_DEV).astype(jnp.int32)
        rows_in = lax.dynamic_slice_in_dim(layer_input, offset, TOK_DEV, 0)
        rows_out = lax.dynamic_slice_in_dim(output_grad, offset, TOK_DEV, 0)
        rows_gate = lax.dynamic_slice_in_dim(gate_delta, offset, TOK_DEV, 0)
        rows_up = lax.dynamic_slice_in_dim(up_delta, offset, TOK_DEV, 0)
        rows_hidden = lax.dynamic_slice_in_dim(hidden, offset, TOK_DEV, 0)
        partials = (transposed_times(rows_in, rows_gate), transposed_times(rows_in, rows_up), transposed_times(rows_hidden, rows_out))
        rounded = tuple(p.astype(jnp.bfloat16) for p in partials)
        rounded = lax.optimization_barrier(rounded)
        return tuple(a + b.astype(jnp.float32) for a, b in zip(totals, rounded)), None

    initial = (jnp.zeros((D, FF), jnp.float32), jnp.zeros((D, FF), jnp.float32), jnp.zeros((FF, D), jnp.float32))
    totals, _ = lax.scan(group_step, initial, jnp.arange(N_DP, dtype=jnp.int32))
    return (input_grad, totals[0].astype(jnp.bfloat16), totals[1].astype(jnp.bfloat16), totals[2].astype(jnp.bfloat16))
```

```python
import jax
import jax.numpy as jnp
from jax import lax
from jax.experimental import pallas as pl
from jax.experimental.pallas import tpu as pltpu
from jax.sharding import PartitionSpec as P

MESH = pl.DeviceIdType.MESH
BF16, F32 = jnp.bfloat16, jnp.float32

D = 4096
F = 896
ROWS = 32
TOK = 512
HALF = 16
BLK = 256
CH = 128
NCH = F // CH


def times_transposed(left, right):
    return lax.dot_general(left, right, (((1,), (1,)), ((), ())), preferred_element_type=F32)


def times(left, right):
    return jnp.dot(left, right, preferred_element_type=F32)


def kernel(
    x_hbm, dy_hbm, gw_hbm, uw_hbm, dw_hbm,
    dx_out, gg_out, ug_out, dg_out,
    buf, sib, wgu, wd, ab, gu, ht, xt, gpart, dpart, r1g, r1d, r2g, r2d, dxs, dxr, gfin, ufin, dfin, dxfin,
    ag_send, ag_recv, w_sem, own_sem, sib_send, sib_recv, ht_send, ht_recv, gu_send, gu_recv,
    s1_send, s1_recv, s2_send, s2_recv, dx_send, dx_recv, out_sem,
):
    dp, t = lax.axis_index("dp"), lax.axis_index("tensor")
    c, xh, z = lax.rem(dp, 2), lax.rem(dp // 2, 2), dp // 4
    y, xl = t // 2, lax.rem(t, 2)
    x = 2 * xh + xl

    def wrap(v):
        return lax.rem(v + 4, 4)

    def dev(pz, px, py, pc):
        return ((pz * 2 + px // 2) * 2 + pc, py * 2 + lax.rem(px, 2))

    sibling = dev(z, x, y, 1 - c)
    z_next, z_prev = dev(wrap(z + 1), x, y, c), dev(wrap(z - 1), x, y, c)

    barrier = pltpu.get_barrier_semaphore()
    greeted = [(dp, lax.rem(t + o, 8)) for o in range(1, 8)]
    greeted += [dev(z, wrap(x + 2 * xl - 1), y, c), z_next, z_prev, sibling]
    for other in greeted:
        pl.semaphore_signal(barrier, inc=1, device_id=other, device_id_type=MESH)

    def rows(px, py, h):
        slot = (px // 2) * 8 + py * 2 + lax.rem(px, 2)
        return pl.ds(pl.multiple_of(slot * ROWS + h * HALF, HALF), HALF)

    own = pl.ds(pl.multiple_of((xh * 8 + t) * ROWS, ROWS), ROWS)
    own_copies = [
        pltpu.make_async_copy(src, buf.at[a, own, :], own_sem.at[a]) for a, src in enumerate((x_hbm, dy_hbm))
    ]
    for copy in own_copies:
        copy.start()
    for j in range(NCH):
        part = pl.ds(j * CH, CH)
        pltpu.make_async_copy(gw_hbm.at[:, part], wgu.at[:, pl.ds(j * 2 * CH, CH)], w_sem.at[0]).start()
        pltpu.make_async_copy(uw_hbm.at[:, part], wgu.at[:, pl.ds(j * 2 * CH + CH, CH)], w_sem.at[0]).start()
    wd_copy = pltpu.make_async_copy(dw_hbm, wd, w_sem.at[1])
    wd_copy.start()
    for copy in own_copies:
        copy.wait()
    pl.semaphore_wait(barrier, len(greeted))

    lo, hi, full = pl.ds(0, D // 2), pl.ds(D // 2, D // 2), pl.ds(0, D)
    offsets = (0, 1, -1, 2)

    def xfer(a, h, idx, du, dv, cols, ring, way):
        u, v = (x, y) if h == 0 else (y, x)
        bu, bv = wrap(u + du), wrap(v + dv)
        tu, tv = (wrap(u + way), v) if ring == 0 else (u, wrap(v + way))
        (bx, by), (tx, ty) = ((bu, bv), (tu, tv)) if h == 0 else ((bv, bu), (tv, tu))
        block = buf.at[a, rows(bx, by, h), cols]
        return pltpu.make_async_remote_copy(
            src_ref=block,
            dst_ref=block,
            send_sem=ag_send.at[a * 2 + h, idx],
            recv_sem=ag_recv.at[a * 2 + h, idx],
            device_id=dev(z, tx, ty, c),
            device_id_type=MESH,
        )

    def first_full(a, h, way, sent):
        return xfer(a, h, 0 if way == 1 else 1, 0 if sent else -way, 0, full, 0, way)

    def first_relay(a, h, way, sent):
        idx, cols = (2, lo) if way == 1 else (3, hi)
        return xfer(a, h, idx, -way if sent else 2, 0, cols, 0, way)

    def second_full(a, h, q, way, sent):
        return xfer(a, h, 4 + 4 * q + (0 if way == 1 else 1), offsets[q], 0 if sent else -way, full, 1, way)

    def second_relay(a, h, q, way, sent):
        idx, cols = (4 + 4 * q + 2, lo) if way == 1 else (4 + 4 * q + 3, hi)
        return xfer(a, h, idx, offsets[q], -way if sent else 2, cols, 1, way)

    def gather_step(a, step):
        for h in range(2):
            if step == 0:
                for way in (1, -1):
                    first_full(a, h, way, True).start()
                for way in (1, -1):
                    second_full(a, h, 0, way, True).start()
            elif step == 1:
                for way, q in ((1, 2), (-1, 1)):
                    first_full(a, h, way, False).wait_recv()
                    first_relay(a, h, way, True).start()
                    for to in (1, -1):
                        second_full(a, h, q, to, True).start()
            elif step == 2:
                for way in (1, -1):
                    second_full(a, h, 0, way, False).wait_recv()
                    second_relay(a, h, 0, way, True).start()
                for way in (1, -1):
                    first_relay(a, h, way, False).wait_recv()
                for to in (1, -1):
                    second_full(a, h, 3, to, True).start()
            elif step == 3:
                for q in (2, 1):
                    for way in (1, -1):
                        second_full(a, h, q, way, False).wait_recv()
                        second_relay(a, h, q, way, True).start()
            elif step == 4:
                for way in (1, -1):
                    second_full(a, h, 3, way, False).wait_recv()
                    second_relay(a, h, 3, way, True).start()
            else:
                for q in range(4):
                    for way in (1, -1):
                        second_relay(a, h, q, way, False).wait_recv()

    def gather_sent(a):
        for h in range(2):
            for way in (1, -1):
                first_full(a, h, way, True).wait_send()
                first_relay(a, h, way, True).wait_send()
                for q in range(4):
                    second_full(a, h, q, way, True).wait_send()
                    second_relay(a, h, q, way, True).wait_send()

    def columns(zb, pc):
        return pl.ds(pl.multiple_of(zb * 1024 + xh * 512 + pc * BLK, BLK), BLK)

    def sibling_columns(a):
        for zb in range(4):
            pltpu.make_async_remote_copy(
                src_ref=buf.at[a, :, columns(zb, 1 - c)],
                dst_ref=sib.at[a, :, pl.ds(zb * BLK, BLK)],
                send_sem=sib_send.at[a],
                recv_sem=sib_recv.at[a],
                device_id=sibling,
                device_id_type=MESH,
            ).start()

    def pre_chunk(j):
        wide = pl.ds(pl.multiple_of(j * 2 * CH, 2 * CH), 2 * CH)
        pre = times(buf[0], wgu[:, wide])
        gate_pre, up_pre = pre[:, :CH], pre[:, CH:]
        sigma = jax.nn.sigmoid(gate_pre)
        swish = gate_pre * sigma
        hidden = swish * up_pre
        ab[:, wide] = jnp.concatenate([up_pre * sigma * (1.0 + gate_pre * (1.0 - sigma)), swish], axis=1)
        part = pl.ds(pl.multiple_of(j * CH, CH), CH)
        ht[part, pl.ds(0, TOK)] = hidden.T.astype(BF16)
        pltpu.make_async_remote_copy(
            src_ref=ht.at[part, pl.ds(0, TOK)],
            dst_ref=ht.at[part, pl.ds(TOK, TOK)],
            send_sem=ht_send.at[0],
            recv_sem=ht_recv.at[0],
            device_id=sibling,
            device_id_type=MESH,
        ).start()

    def delta_chunk(j, width):
        n = width * CH
        hg = times_transposed(buf[1], wd[pl.ds(pl.multiple_of(j * CH, CH), n), :])
        for w in range(width):
            wide = pl.ds(pl.multiple_of((j + w) * 2 * CH, 2 * CH), 2 * CH)
            part = hg[:, w * CH : (w + 1) * CH]
            gu[pl.ds(0, TOK), wide] = (jnp.concatenate([part, part], axis=1) * ab[:, wide]).astype(BF16)
        wide = pl.ds(pl.multiple_of(j * 2 * CH, 2 * CH), 2 * n)
        pltpu.make_async_remote_copy(
            src_ref=gu.at[pl.ds(0, TOK), wide],
            dst_ref=gu.at[pl.ds(TOK, TOK), wide],
            send_sem=gu_send.at[0],
            recv_sem=gu_recv.at[0],
            device_id=sibling,
            device_id_type=MESH,
        ).start()

    def whole(ref, sem):
        return pltpu.make_async_copy(ref, ref, sem)

    gather_step(0, 0)
    gather_step(0, 1)
    gather_step(0, 2)
    gather_step(1, 0)
    gather_step(0, 3)
    gather_step(1, 1)
    gather_step(0, 4)
    gather_step(1, 2)
    gather_step(0, 5)
    sibling_columns(0)
    whole(wgu, w_sem.at[0]).wait()

    @pl.loop(0, 3)
    def _(j):
        pre_chunk(j)

    gather_step(1, 3)

    @pl.loop(3, NCH)
    def _(j):
        pre_chunk(j)

    gather_step(1, 4)

    whole(sib.at[0], sib_recv.at[0]).wait()

    @pl.loop(0, 4)
    def _(k):
        zb = lax.rem(z + k, 4)
        xt[k, :, pl.ds(0, TOK)] = buf[0, :, columns(zb, c)].T
        xt[k, :, pl.ds(TOK, TOK)] = sib[0, :, pl.ds(pl.multiple_of(zb * BLK, BLK), BLK)].T

    gather_step(1, 5)
    sibling_columns(1)
    wd_copy.wait()

    @pl.loop(0, NCH // 2)
    def _(j):
        delta_chunk(2 * j, 2)

    delta_chunk(NCH - 1, 1)

    def down_part(k):
        zb = lax.rem(z + k, 4)
        total = times(ht[:, pl.ds(0, TOK)], buf[1, :, columns(zb, c)])
        total += times(ht[:, pl.ds(TOK, TOK)], sib[1, :, pl.ds(pl.multiple_of(zb * BLK, BLK), BLK)])
        dpart[k] = total.astype(BF16)

    def gu_part(k):
        @pl.loop(0, NCH)
        def _(j):
            wide = pl.ds(pl.multiple_of(j * 2 * CH, 2 * CH), 2 * CH)
            gpart[k, :, wide] = times(xt[k], gu[:, wide]).astype(BF16)

    def first(part, received, i, way):
        size = part.shape[1] // 2
        half = pl.ds(0 if way == 1 else size, size)
        side = 0 if way == 1 else 1
        return pltpu.make_async_remote_copy(
            src_ref=part.at[2, half, :],
            dst_ref=received.at[side],
            send_sem=s1_send.at[i, side],
            recv_sem=s1_recv.at[i, side],
            device_id=z_next if way == 1 else z_prev,
            device_id_type=MESH,
        )

    def second(part, received, i, way):
        side = 0 if way == 1 else 1
        return pltpu.make_async_remote_copy(
            src_ref=part.at[1 if way == 1 else 3],
            dst_ref=received.at[side],
            send_sem=s2_send.at[i, side],
            recv_sem=s2_recv.at[i, side],
            device_id=z_next if way == 1 else z_prev,
            device_id_type=MESH,
        )

    def add_first(part, received, i):
        size = part.shape[1] // 2
        for way in (1, -1):
            side, k = (0, 1) if way == 1 else (1, 3)
            first(part, received, i, way).wait_recv()
            half = pl.ds(side * size, size)
            part[k, half, :] = (part[k, half, :].astype(F32) + received[side].astype(F32)).astype(BF16)
            second(part, received_2[i], i, way).start()

    received_2 = (r2d, r2g)
    whole(sib.at[1], sib_recv.at[1]).wait()
    whole(ht.at[:, pl.ds(TOK, TOK)], ht_recv.at[0]).wait()
    down_part(2)
    for way in (1, -1):
        first(dpart, r1d, 0, way).start()
    whole(gu.at[pl.ds(TOK, TOK), :], gu_recv.at[0]).wait()
    gu_part(2)
    for way in (1, -1):
        first(gpart, r1g, 1, way).start()
    down_part(1)
    down_part(3)
    add_first(dpart, r1d, 0)

    @pl.loop(0, D // 256)
    def _(n):
        strip = pl.ds(pl.multiple_of(n * 256, 256), 256)
        mine = gu[pl.ds(pl.multiple_of(xh * 256, 256), 256), :]
        dxs[:, strip] = times_transposed(mine, wgu[strip, :]).astype(BF16)

    def dx_rows(s):
        return pl.ds(pl.multiple_of(s * ROWS, ROWS), ROWS)

    def dx_copy(o):
        to = lax.rem(t + o, 8)
        return pltpu.make_async_remote_copy(
            src_ref=dxs.at[dx_rows(to), :],
            dst_ref=dxr.at[dx_rows(t), :],
            send_sem=dx_send.at[o],
            recv_sem=dx_recv.at[o],
            device_id=(dp, to),
            device_id_type=MESH,
        )

    for o in range(1, 8):
        dx_copy(o).start()

    gu_part(1)
    gu_part(3)
    add_first(gpart, r1g, 1)
    down_part(0)
    gu_part(0)

    for way in (1, -1):
        second(dpart, r2d, 0, way).wait_recv()
    dfin[...] = (dpart[0].astype(F32) + r2d[0].astype(F32) + r2d[1].astype(F32)).astype(BF16)
    outs = [pltpu.make_async_copy(dfin, dg_out, out_sem.at[0])]
    outs[0].start()

    for o in range(1, 8):
        dx_copy(o).wait_recv()
    total = dxs[dx_rows(t), :].astype(F32)
    for o in range(1, 8):
        total += dxr[dx_rows(lax.rem(t + 8 - o, 8)), :].astype(F32)
    dxfin[...] = total.astype(BF16)
    outs.append(pltpu.make_async_copy(dxfin, dx_out, out_sem.at[1]))
    outs[1].start()

    for way in (1, -1):
        second(gpart, r2g, 1, way).wait_recv()

    @pl.loop(0, NCH)
    def _(j):
        wide = pl.ds(pl.multiple_of(j * 2 * CH, 2 * CH), 2 * CH)
        part = pl.ds(pl.multiple_of(j * CH, CH), CH)
        total = gpart[0, :, wide].astype(F32) + r2g[0, :, wide].astype(F32) + r2g[1, :, wide].astype(F32)
        gfin[:, part] = total[:, :CH].astype(BF16)
        ufin[:, part] = total[:, CH:].astype(BF16)

    outs.append(pltpu.make_async_copy(gfin, gg_out, out_sem.at[2]))
    outs.append(pltpu.make_async_copy(ufin, ug_out, out_sem.at[3]))
    outs[2].start()
    outs[3].start()

    for a in range(2):
        gather_sent(a)
        whole(sib.at[a], sib_send.at[a]).wait()
    whole(ht.at[:, pl.ds(0, TOK)], ht_send.at[0]).wait()
    whole(gu.at[pl.ds(0, TOK), :], gu_send.at[0]).wait()
    for way in (1, -1):
        for part, r1, r2, i in ((dpart, r1d, r2d, 0), (gpart, r1g, r2g, 1)):
            first(part, r1, i, way).wait_send()
            second(part, r2, i, way).wait_send()
    for o in range(1, 8):
        dx_copy(o).wait_send()
    for copy in outs:
        copy.wait()


def per_device(layer_input, output_grad, gate_weight, up_weight, down_weight):
    dma = pltpu.SemaphoreType.DMA
    vmem = pltpu.VMEM
    return pl.pallas_call(
        kernel,
        out_shape=(
            jax.ShapeDtypeStruct((ROWS, D), BF16),
            jax.ShapeDtypeStruct((BLK, F), BF16),
            jax.ShapeDtypeStruct((BLK, F), BF16),
            jax.ShapeDtypeStruct((F, BLK), BF16),
        ),
        in_specs=[pl.BlockSpec(memory_space=pl.ANY)] * 5,
        out_specs=[pl.BlockSpec(memory_space=pl.ANY)] * 4,
        scratch_shapes=[
            vmem((2, TOK, D), BF16),
            vmem((2, TOK, 4 * BLK), BF16),
            vmem((D, 2 * F), BF16),
            vmem((F, D), BF16),
            vmem((TOK, 2 * F), F32),
            vmem((2 * TOK, 2 * F), BF16),
            vmem((F, 2 * TOK), BF16),
            vmem((4, BLK, 2 * TOK), BF16),
            vmem((4, BLK, 2 * F), BF16),
            vmem((4, F, BLK), BF16),
            vmem((2, BLK // 2, 2 * F), BF16),
            vmem((2, F // 2, BLK), BF16),
            vmem((2, BLK, 2 * F), BF16),
            vmem((2, F, BLK), BF16),
            vmem((8 * ROWS, D), BF16),
            vmem((8 * ROWS, D), BF16),
            vmem((BLK, F), BF16),
            vmem((BLK, F), BF16),
            vmem((F, BLK), BF16),
            vmem((ROWS, D), BF16),
            dma((4, 20)),
            dma((4, 20)),
            dma((2,)),
            dma((2,)),
            dma((2,)),
            dma((2,)),
            dma((1,)),
            dma((1,)),
            dma((1,)),
            dma((1,)),
            dma((2, 2)),
            dma((2, 2)),
            dma((2, 2)),
            dma((2, 2)),
            dma((8,)),
            dma((8,)),
            dma((4,)),
        ],
        compiler_params=pltpu.CompilerParams(
            collective_id=0, has_side_effects=True, vmem_limit_bytes=63 * 1024 * 1024
        ),
        cost_estimate=pl.CostEstimate(flops=21 * 10**9, bytes_accessed=26 * 10**6, transcendentals=10**6),
    )(layer_input, output_grad, gate_weight, up_weight, down_weight)


def solution(mesh):
    placed = (
        P(("dp", "tensor"), None),
        P(("dp", "tensor"), None),
        P(None, "tensor"),
        P(None, "tensor"),
        P("tensor", None),
    )
    return jax.shard_map(
        per_device,
        mesh=mesh,
        in_specs=placed,
        out_specs=(
            P(("dp", "tensor"), None),
            P("dp", "tensor"),
            P("dp", "tensor"),
            P("tensor", "dp"),
        ),
        check_vma=False,
    )
```

```python
import jax
import jax.numpy as jnp
from jax import lax
from jax.experimental import pallas as pl
from jax.experimental.pallas import tpu as pltpu
from jax.sharding import PartitionSpec as P

MESH = pl.DeviceIdType.MESH
BF16, F32 = jnp.bfloat16, jnp.float32

D = 4096
F = 896
ROWS = 32
TOK = 512
HALF = 16
BLK = 256
CH = 128
NCH = F // CH
WIDE = D // 2


def times_transposed(left, right):
    return lax.dot_general(left, right, (((1,), (1,)), ((), ())), preferred_element_type=F32)


def times(left, right):
    return jnp.dot(left, right, preferred_element_type=F32)


def kernel(
    x_hbm, dy_hbm, gw_hbm, uw_hbm, dw_hbm,
    dx_out, gg_out, ug_out, dg_out,
    buf, sib, wgu, wd, ab, hga, gu, ht, xt, dpart, gpart, r1d, r1g, r2d, r2g, dxs, dxr, gfin, ufin,
    ag_send, ag_recv, w_sem, own_sem, sib_send, sib_recv, ht_send, ht_recv, gu_send, gu_recv,
    s1_send, s1_recv, s2_send, s2_recv, dx_send, dx_recv, out_sem,
):
    dp, t = lax.axis_index("dp"), lax.axis_index("tensor")
    c, xh, z = lax.rem(dp, 2), lax.rem(dp // 2, 2), dp // 4
    y, xl = t // 2, lax.rem(t, 2)
    x = 2 * xh + xl

    def wrap(v):
        return lax.rem(v + 4, 4)

    def dev(pz, px, py, pc):
        return ((pz * 2 + px // 2) * 2 + pc, py * 2 + lax.rem(px, 2))

    sibling = dev(z, x, y, 1 - c)
    z_next, z_prev = dev(wrap(z + 1), x, y, c), dev(wrap(z - 1), x, y, c)

    barrier = pltpu.get_barrier_semaphore()
    greeted = [(dp, lax.rem(t + o, 8)) for o in range(1, 8)]
    greeted += [dev(z, wrap(x + 2 * xl - 1), y, c), z_next, z_prev, sibling]
    for other in greeted:
        pl.semaphore_signal(barrier, inc=1, device_id=other, device_id_type=MESH)

    def rows(px, py, h):
        slot = (px // 2) * 8 + py * 2 + lax.rem(px, 2)
        return pl.ds(pl.multiple_of(slot * ROWS + h * HALF, HALF), HALF)

    own = pl.ds(pl.multiple_of((xh * 8 + t) * ROWS, ROWS), ROWS)
    own_copies = [
        pltpu.make_async_copy(src, buf.at[a, own, :], own_sem.at[a]) for a, src in enumerate((x_hbm, dy_hbm))
    ]
    for copy in own_copies:
        copy.start()
    for copy in own_copies:
        copy.wait()
    pl.semaphore_wait(barrier, len(greeted))

    wd_copy = pltpu.make_async_copy(dw_hbm, wd, w_sem.at[1])

    def load_weights():
        for j in range(NCH):
            part = pl.ds(j * CH, CH)
            pltpu.make_async_copy(gw_hbm.at[:, part], wgu.at[:, pl.ds(j * 2 * CH, CH)], w_sem.at[0]).start()
            pltpu.make_async_copy(uw_hbm.at[:, part], wgu.at[:, pl.ds(j * 2 * CH + CH, CH)], w_sem.at[0]).start()
        wd_copy.start()

    far = lax.rem(z + 2, 4)
    pair = far // 2
    units = ((0, 0, WIDE), (0, WIDE, WIDE), (1, far * 1024, 1024), (1, (4 * pair + 1 - far) * 1024, 1024), (1, (1 - pair) * WIDE, WIDE))
    offsets = (0, 1, -1, 2)

    def aligned(start, size):
        return pl.ds(start if isinstance(start, int) else pl.multiple_of(start, 256), size)

    def unit_columns(g, part):
        _, begin, size = units[g]
        return aligned(begin, size) if part is None else aligned(begin + part * (size // 2), size // 2)

    def xfer(g, h, idx, du, dv, part, ring, way):
        u, v = (x, y) if h == 0 else (y, x)
        bu, bv = wrap(u + du), wrap(v + dv)
        tu, tv = (wrap(u + way), v) if ring == 0 else (u, wrap(v + way))
        (bx, by), (tx, ty) = ((bu, bv), (tu, tv)) if h == 0 else ((bv, bu), (tv, tu))
        block = buf.at[units[g][0], rows(bx, by, h), unit_columns(g, part)]
        return pltpu.make_async_remote_copy(
            src_ref=block,
            dst_ref=block,
            send_sem=ag_send.at[g * 2 + h],
            recv_sem=ag_recv.at[g * 2 + h, idx],
            device_id=dev(z, tx, ty, c),
            device_id_type=MESH,
        )

    def first_full(g, h, way, sent):
        return xfer(g, h, 0 if way == 1 else 1, 0 if sent else -way, 0, None, 0, way)

    def first_relay(g, h, way, sent):
        idx, part = (2, 0) if way == 1 else (3, 1)
        return xfer(g, h, idx, -way if sent else 2, 0, part, 0, way)

    def second_full(g, h, q, way, sent):
        return xfer(g, h, 4 + 4 * q + (0 if way == 1 else 1), offsets[q], 0 if sent else -way, None, 1, way)

    def second_relay(g, h, q, way, sent):
        idx, part = (4 + 4 * q + 2, 0) if way == 1 else (4 + 4 * q + 3, 1)
        return xfer(g, h, idx, offsets[q], -way if sent else 2, part, 1, way)

    def gather(*acts):
        for g, h, what in acts:
            if what == 0:
                for way in (1, -1):
                    first_full(g, h, way, True).start()
                for way in (1, -1):
                    second_full(g, h, 0, way, True).start()
            elif what < 3:
                way, q = ((1, 2), (-1, 1))[what - 1]
                first_full(g, h, way, False).wait_recv()
                first_relay(g, h, way, True).start()
                for to in (1, -1):
                    second_full(g, h, q, to, True).start()
            elif what == 3:
                for way in (1, -1):
                    first_relay(g, h, way, False).wait_recv()
                for to in (1, -1):
                    second_full(g, h, 3, to, True).start()
            elif what < 12:
                q, way = (what - 4) // 2, 1 - 2 * (what % 2)
                second_full(g, h, q, way, False).wait_recv()
                second_relay(g, h, q, way, True).start()
            else:
                for q in range(4):
                    for way in (1, -1):
                        second_relay(g, h, q, way, False).wait_recv()

    def whole(ref, sem):
        return pltpu.make_async_copy(ref, ref, sem)

    def columns(zb, pc):
        return pl.ds(pl.multiple_of(zb * 1024 + xh * 512 + pc * BLK, BLK), BLK)

    def own_strip(zb):
        return pl.ds(pl.multiple_of(zb * BLK, BLK), BLK)

    def strips(g):
        a, begin, size = units[g]
        return [begin // 1024 + i for i in range(size // 1024)]

    def sibling_columns(g):
        for zb in strips(g):
            pltpu.make_async_remote_copy(
                src_ref=buf.at[units[g][0], :, columns(zb, 1 - c)],
                dst_ref=sib.at[units[g][0], :, own_strip(zb)],
                send_sem=sib_send.at[g],
                recv_sem=sib_recv.at[g],
                device_id=sibling,
                device_id_type=MESH,
            ).start()

    def sibling_wait(g, sem):
        a, begin, size = units[g]
        whole(sib.at[a, :, aligned(begin // 4, size // 4)], sem.at[g]).wait()

    def chunk(j):
        return pl.ds(pl.multiple_of(j * 2 * CH, 2 * CH), 2 * CH)

    pieces = ((0, 3), (3, 5), (5, 7))

    def pre_first(piece):
        j0, j1 = pieces[piece]
        if piece == 0:
            whole(wgu, w_sem.at[0]).wait()
        at = pl.ds(j0 * 2 * CH, (j1 - j0) * 2 * CH)
        ab[:, at] = times(buf[0, :, :WIDE], wgu[:WIDE, at])

    def pre_second(piece):
        j0, j1 = pieces[piece]
        at = pl.ds(j0 * 2 * CH, (j1 - j0) * 2 * CH)
        pre = ab[:, at] + times(buf[0, :, WIDE:], wgu[WIDE:, at])
        for j in range(j0, j1):
            begin = (j - j0) * 2 * CH
            gate_pre, up_pre = pre[:, begin : begin + CH], pre[:, begin + CH : begin + 2 * CH]
            sigma = jax.nn.sigmoid(gate_pre)
            swish = gate_pre * sigma
            hidden = swish * up_pre
            ab[:, chunk(j)] = jnp.concatenate([up_pre * sigma * (1.0 + gate_pre * (1.0 - sigma)), swish], axis=1)
            ht[pl.ds(j * CH, CH), pl.ds(0, TOK)] = hidden.T.astype(BF16)
        part = pl.ds(j0 * CH, (j1 - j0) * CH)
        pltpu.make_async_remote_copy(
            src_ref=ht.at[part, pl.ds(0, TOK)],
            dst_ref=ht.at[part, pl.ds(TOK, TOK)],
            send_sem=ht_send.at[0],
            recv_sem=ht_recv.at[0],
            device_id=sibling,
            device_id_type=MESH,
        ).start()

    def first_hidden_grad(piece):
        at, half = ((pl.ds(0, 512), pl.ds(512, 384))[piece], aligned(pair * WIDE, WIDE))
        if piece == 0:
            wd_copy.wait()
        hga[:, at] = times_transposed(buf[1, :, half], wd[at, half])

    def delta_size(i):
        return min(2, NCH - 2 * i) * CH

    def delta_chunk(i):
        at, half = pl.ds(i * 2 * CH, delta_size(i)), aligned((1 - pair) * WIDE, WIDE)
        hg = hga[:, at] + times_transposed(buf[1, :, half], wd[at, half])
        for w in range(delta_size(i) // CH):
            part = hg[:, w * CH : (w + 1) * CH]
            to = chunk(2 * i + w)
            gu[pl.ds(0, TOK), to] = (jnp.concatenate([part, part], axis=1) * ab[:, to]).astype(BF16)
        delta_copy(i).start()

    def delta_columns(i):
        return pl.ds(i * 4 * CH, 2 * delta_size(i))

    def delta_copy(i):
        return pltpu.make_async_remote_copy(
            src_ref=gu.at[pl.ds(0, TOK), delta_columns(i)],
            dst_ref=gu.at[pl.ds(TOK, TOK), delta_columns(i)],
            send_sem=gu_send.at[i],
            recv_sem=gu_recv.at[i],
            device_id=sibling,
            device_id_type=MESH,
        )

    def transposed_x():
        sibling_wait(0, sib_recv)
        sibling_wait(1, sib_recv)

        @pl.loop(0, 4)
        def _(k):
            zb = lax.rem(z + k, 4)
            xt[k, :, pl.ds(0, TOK)] = buf[0, :, columns(zb, c)].T
            xt[k, :, pl.ds(TOK, TOK)] = sib[0, :, own_strip(zb)].T

    def down_part(k):
        zb = lax.rem(z + k, 4)
        total = times(ht[:, pl.ds(0, TOK)], buf[1, :, columns(zb, c)])
        total += times(ht[:, pl.ds(TOK, TOK)], sib[1, :, own_strip(zb)])
        dpart[k] = total.astype(BF16)

    def gu_part(i, k):
        gpart[k, :, delta_columns(i)] = times(xt[k], gu[:, delta_columns(i)]).astype(BF16)

    sums = [(dpart, r1d, r2d, pl.ds(0, BLK))] + [(gpart, r1g, r2g, delta_columns(i)) for i in range(4)]

    def z_side(side):
        return dev(wrap(z + 1 - 2 * side), x, y, c)

    def half_of(i, side):
        size = sums[i][0].shape[1] // 2
        return pl.ds(side * size if isinstance(side, int) else pl.multiple_of(side * size, size), size)

    def first(i, side):
        part, received, _, cols = sums[i]
        return pltpu.make_async_remote_copy(
            src_ref=part.at[2, half_of(i, side), cols],
            dst_ref=received.at[side, :, cols],
            send_sem=s1_send.at[i, side],
            recv_sem=s1_recv.at[i, side],
            device_id=z_side(side),
            device_id_type=MESH,
        )

    def second(i, side):
        part, _, received, cols = sums[i]
        return pltpu.make_async_remote_copy(
            src_ref=part.at[1 + 2 * side, :, cols],
            dst_ref=received.at[side, :, cols],
            send_sem=s2_send.at[i, side],
            recv_sem=s2_recv.at[i, side],
            device_id=z_side(side),
            device_id_type=MESH,
        )

    def add_first(i, side):
        part, received, _, cols = sums[i]
        first(i, side).wait_recv()
        k, half = 1 + 2 * side, half_of(i, side)
        part[k, half, cols] = (part[k, half, cols].astype(F32) + received[side, :, cols].astype(F32)).astype(BF16)
        second(i, side).start()

    def add_second(i):
        part, _, received, cols = sums[i]
        for side in range(2):
            second(i, side).wait_recv()
        total = part[0, :, cols].astype(F32) + received[0, :, cols].astype(F32)
        return total + received[1, :, cols].astype(F32)

    side_a = 1 - lax.rem(z, 2)
    side_b = 1 - side_a

    def down_far():
        whole(ht.at[:, pl.ds(TOK, TOK)], ht_recv.at[0]).wait()
        sibling_wait(2, sib_recv)
        down_part(2)
        first(0, 0).start()
        first(0, 1).start()

    def down_near():
        sibling_wait(3, sib_recv)
        down_part(1 + 2 * side_a)

    def gu_far(i):
        delta_copy(i).wait_recv()
        gu_part(i, 2)
        first(1 + i, 0).start()
        first(1 + i, 1).start()

    def gu_near(i):
        for side in range(2):
            gu_part(i, 1 + 2 * side)
        for side in range(2):
            add_first(1 + i, side)

    def dx_rows(s):
        return pl.ds(pl.multiple_of(s * ROWS, ROWS), ROWS)

    def dx_copy(o, half):
        to = lax.rem(t + o, 8)
        at = pl.ds(half * WIDE, WIDE)
        return pltpu.make_async_remote_copy(
            src_ref=dxs.at[dx_rows(to), at],
            dst_ref=dxr.at[dx_rows(t), at],
            send_sem=dx_send.at[half, o],
            recv_sem=dx_recv.at[half, o],
            device_id=(dp, to),
            device_id_type=MESH,
        )

    def dx_part(half):
        mine = gu[pl.ds(pl.multiple_of(xh * 256, 256), 256), :]
        for n in range(2):
            strip = pl.ds(half * WIDE + n * 1024, 1024)
            dxs[:, strip] = times_transposed(mine, wgu[strip, :]).astype(BF16)

        for o in range(1, 8):
            dx_copy(o, half).start()

    gather((0, 0, 0), (0, 1, 0), (1, 1, 0), (1, 0, 0))
    load_weights()
    gather((0, 0, 1), (0, 0, 2), (0, 0, 4), (0, 0, 5), (0, 1, 4), (0, 1, 5), (0, 1, 1), (0, 1, 2), (1, 1, 4))
    gather((1, 1, 5), (1, 1, 1), (1, 1, 2), (1, 0, 1), (1, 0, 2), (1, 0, 4), (1, 0, 5), (0, 0, 3), (0, 0, 8))
    gather((0, 0, 9), (0, 1, 8), (0, 1, 9), (0, 0, 6), (0, 0, 7), (2, 0, 0), (0, 1, 6), (0, 1, 7), (0, 1, 3))
    gather((2, 1, 0), (1, 1, 3), (1, 1, 8), (1, 1, 9), (1, 0, 8), (1, 0, 9), (3, 1, 0), (1, 1, 6), (1, 1, 7))
    gather((1, 0, 6), (1, 0, 7), (1, 0, 3), (3, 0, 0), (4, 0, 0), (0, 0, 10), (0, 0, 11), (2, 0, 1), (0, 1, 10))
    gather((0, 1, 11), (2, 0, 4), (2, 0, 5), (2, 0, 2), (2, 1, 4), (2, 1, 5), (2, 1, 1), (2, 1, 2), (1, 1, 10))
    gather((1, 1, 11), (3, 1, 1), (3, 1, 2), (3, 1, 4), (3, 1, 5), (4, 1, 0), (1, 0, 10), (1, 0, 11), (3, 0, 4))
    gather((3, 0, 5), (3, 0, 1), (3, 0, 2), (4, 0, 1), (4, 0, 4), (0, 0, 12), (4, 0, 5), (0, 1, 12))
    sibling_columns(0)
    pre_first(0)
    gather((2, 0, 8), (2, 0, 9), (2, 0, 3), (2, 1, 8), (2, 1, 9), (2, 0, 6), (2, 0, 7), (2, 1, 6), (1, 1, 12))
    gather((2, 1, 7), (2, 1, 3), (3, 1, 3), (4, 0, 2))
    pre_first(1)
    gather((3, 1, 8), (1, 0, 12))
    sibling_columns(1)
    gather((3, 1, 9), (3, 1, 6), (3, 1, 7), (4, 1, 1), (4, 1, 2))
    pre_first(2)
    gather((3, 0, 8), (3, 0, 9), (3, 0, 3), (3, 0, 6), (3, 0, 7), (4, 1, 4), (4, 1, 5))
    pre_second(0)
    gather((2, 1, 11), (2, 1, 10), (2, 0, 10), (2, 0, 11), (3, 1, 11), (3, 1, 10), (4, 0, 8), (4, 0, 9), (4, 0, 3))
    pre_second(1)
    gather((4, 1, 8), (4, 1, 9), (4, 0, 6), (4, 0, 7))
    pre_second(2)
    gather((3, 0, 10), (3, 0, 11), (4, 1, 3), (2, 1, 12), (4, 1, 6), (2, 0, 12))
    sibling_columns(2)
    gather((4, 1, 7))
    transposed_x()
    gather((3, 1, 12))
    down_far()
    gather((4, 0, 10), (4, 0, 11), (3, 0, 12))
    sibling_columns(3)
    first_hidden_grad(0)
    gather((4, 1, 10), (4, 1, 11))
    first_hidden_grad(1)
    gather((4, 0, 12))
    down_near()
    gather((4, 1, 12))
    sibling_columns(4)
    delta_chunk(0)
    delta_chunk(1)
    add_first(0, side_a)
    gu_far(0)
    delta_chunk(2)
    gu_far(1)
    delta_chunk(3)
    sibling_wait(4, sib_recv)
    down_part(1 + 2 * side_b)
    add_first(0, side_b)
    gu_far(2)
    gu_far(3)
    dx_part(0)
    gu_near(0)
    dx_part(1)
    gu_near(1)
    gu_near(2)
    gu_near(3)
    down_part(0)
    for i in range(4):
        gu_part(i, 0)

    for i in range(5):
        for side in range(2):
            first(i, side).wait_send()
    outs = [
        pltpu.make_async_copy(dpart.at[2], dg_out, out_sem.at[0]),
        pltpu.make_async_copy(dxs.at[dx_rows(t), :], dx_out, out_sem.at[1]),
        pltpu.make_async_copy(gfin, gg_out, out_sem.at[2]),
        pltpu.make_async_copy(ufin, ug_out, out_sem.at[3]),
    ]
    dpart[2] = add_second(0).astype(BF16)
    outs[0].start()

    def grads(i):
        total = add_second(1 + i)
        for w in range(delta_size(i) // CH):
            at = pl.ds((2 * i + w) * CH, CH)
            gfin[:, at] = total[:, 2 * w * CH : (2 * w + 1) * CH].astype(BF16)
            ufin[:, at] = total[:, (2 * w + 1) * CH : (2 * w + 2) * CH].astype(BF16)

    grads(0)
    grads(1)
    for half in range(2):
        for o in range(1, 8):
            dx_copy(o, half).wait_recv()
    total = dxs[dx_rows(t), :].astype(F32)
    for o in range(1, 8):
        total += dxr[dx_rows(lax.rem(t + o, 8)), :].astype(F32)
    dxs[dx_rows(t), :] = total.astype(BF16)
    outs[1].start()
    grads(2)
    grads(3)
    outs[2].start()
    outs[3].start()

    for g, (_, _, size) in enumerate(units):
        for h in range(2):
            whole(buf.at[0, pl.ds(0, 15 * HALF), pl.ds(0, size)], ag_send.at[g * 2 + h]).wait()
        sibling_wait(g, sib_send)
    whole(ht.at[:, pl.ds(0, TOK)], ht_send.at[0]).wait()
    for i in range(4):
        delta_copy(i).wait_send()
    for i in range(5):
        for side in range(2):
            second(i, side).wait_send()
    for half in range(2):
        for o in range(1, 8):
            dx_copy(o, half).wait_send()
    for copy in outs:
        copy.wait()


def hand_on(*refs):
    for given, result in zip(refs[:4], refs[4:]):
        result[...] = given[...]


def per_device(layer_input, output_grad, gate_weight, up_weight, down_weight):
    dma = pltpu.SemaphoreType.DMA
    vmem = pltpu.VMEM
    results = (
        jax.ShapeDtypeStruct((ROWS, D), BF16),
        jax.ShapeDtypeStruct((BLK, F), BF16),
        jax.ShapeDtypeStruct((BLK, F), BF16),
        jax.ShapeDtypeStruct((F, BLK), BF16),
    )
    found = pl.pallas_call(
        kernel,
        out_shape=results,
        in_specs=[pl.BlockSpec(memory_space=pl.ANY)] * 5,
        out_specs=[pl.BlockSpec(memory_space=pl.ANY)] * 4,
        scratch_shapes=[
            vmem((2, TOK, D), BF16),
            vmem((2, TOK, 4 * BLK), BF16),
            vmem((D, 2 * F), BF16),
            vmem((F, D), BF16),
            vmem((TOK, 2 * F), F32),
            vmem((TOK, F), F32),
            vmem((2 * TOK, 2 * F), BF16),
            vmem((F, 2 * TOK), BF16),
            vmem((4, BLK, 2 * TOK), BF16),
            vmem((4, F, BLK), BF16),
            vmem((4, BLK, 2 * F), BF16),
            vmem((2, F // 2, BLK), BF16),
            vmem((2, BLK // 2, 2 * F), BF16),
            vmem((2, F, BLK), BF16),
            vmem((2, BLK, 2 * F), BF16),
            vmem((8 * ROWS, D), BF16),
            vmem((8 * ROWS, D), BF16),
            vmem((BLK, F), BF16),
            vmem((BLK, F), BF16),
            dma((10,)),
            dma((10, 20)),
            dma((2,)),
            dma((2,)),
            dma((5,)),
            dma((5,)),
            dma((1,)),
            dma((1,)),
            dma((4,)),
            dma((4,)),
            dma((5, 2)),
            dma((5, 2)),
            dma((5, 2)),
            dma((5, 2)),
            dma((2, 8)),
            dma((2, 8)),
            dma((4,)),
        ],
        compiler_params=pltpu.CompilerParams(
            collective_id=0, has_side_effects=True, vmem_limit_bytes=63 * 1024 * 1024
        ),
        cost_estimate=pl.CostEstimate(flops=21 * 10**9, bytes_accessed=26 * 10**6, transcendentals=10**6),
    )(layer_input, output_grad, gate_weight, up_weight, down_weight)
    return pl.pallas_call(
        hand_on,
        out_shape=results,
        in_specs=[pl.BlockSpec(memory_space=pltpu.VMEM)] * 4,
        out_specs=[pl.BlockSpec(memory_space=pltpu.VMEM)] * 4,
        cost_estimate=pl.CostEstimate(flops=0, bytes_accessed=4 * 10**6, transcendentals=0),
    )(*found)


def solution(mesh):
    placed = (
        P(("dp", "tensor"), None),
        P(("dp", "tensor"), None),
        P(None, "tensor"),
        P(None, "tensor"),
        P("tensor", None),
    )
    return jax.shard_map(
        per_device,
        mesh=mesh,
        in_specs=placed,
        out_specs=(
            P(("dp", "tensor"), None),
            P("dp", "tensor"),
            P("dp", "tensor"),
            P("tensor", "dp"),
        ),
        check_vma=False,
    )
```

```python
import jax
import jax.numpy as jnp
from jax import lax
from jax.experimental import pallas as pl
from jax.experimental.pallas import tpu as pltpu
from jax.sharding import PartitionSpec as P

MESH = pl.DeviceIdType.MESH
BF16, F32 = jnp.bfloat16, jnp.float32

D = 4096
F = 896
ROWS = 32
TOK = 512
HALF = 16
BLK = 256
CH = 128
NCH = F // CH
WIDE = D // 2


def times_transposed(left, right):
    return lax.dot_general(left, right, (((1,), (1,)), ((), ())), preferred_element_type=F32)


def times(left, right):
    return jnp.dot(left, right, preferred_element_type=F32)


def kernel(
    x_hbm, dy_hbm, gw_hbm, uw_hbm, dw_hbm,
    dx_out, gg_out, ug_out, dg_out,
    buf, sib, wgu, wd, ab, hga, gu, ht, xt, dpart, gpart, r1d, r1g, r2d, r2g, dxs, dxr, gfin, ufin,
    ag_send, ag_recv, w_sem, own_sem, sib_send, sib_recv, ht_send, ht_recv, gu_send, gu_recv,
    s1_send, s1_recv, s2_send, s2_recv, dx_send, dx_recv, out_sem,
):
    dp, t = lax.axis_index("dp"), lax.axis_index("tensor")
    c, xh, z = lax.rem(dp, 2), lax.rem(dp // 2, 2), dp // 4
    y, xl = t // 2, lax.rem(t, 2)
    x = 2 * xh + xl

    def wrap(v):
        return lax.rem(v + 4, 4)

    def dev(pz, px, py, pc):
        return ((pz * 2 + px // 2) * 2 + pc, py * 2 + lax.rem(px, 2))

    sibling = dev(z, x, y, 1 - c)
    z_next, z_prev = dev(wrap(z + 1), x, y, c), dev(wrap(z - 1), x, y, c)

    barrier = pltpu.get_barrier_semaphore()
    greeted = [(dp, lax.rem(t + o, 8)) for o in range(1, 8)]
    greeted += [dev(z, wrap(x + 2 * xl - 1), y, c), z_next, z_prev, sibling]
    for other in greeted:
        pl.semaphore_signal(barrier, inc=1, device_id=other, device_id_type=MESH)

    def rows(px, py, h):
        slot = (px // 2) * 8 + py * 2 + lax.rem(px, 2)
        return pl.ds(pl.multiple_of(slot * ROWS + h * HALF, HALF), HALF)

    own = pl.ds(pl.multiple_of((xh * 8 + t) * ROWS, ROWS), ROWS)
    own_copies = [
        pltpu.make_async_copy(src, buf.at[a, own, :], own_sem.at[a]) for a, src in enumerate((x_hbm, dy_hbm))
    ]
    for copy in own_copies:
        copy.start()
    for copy in own_copies:
        copy.wait()
    pl.semaphore_wait(barrier, len(greeted))

    wd_copy = pltpu.make_async_copy(dw_hbm, wd, w_sem.at[1])

    def load_weights():
        for j in range(NCH):
            part = pl.ds(j * CH, CH)
            pltpu.make_async_copy(gw_hbm.at[:, part], wgu.at[:, pl.ds(j * 2 * CH, CH)], w_sem.at[0]).start()
            pltpu.make_async_copy(uw_hbm.at[:, part], wgu.at[:, pl.ds(j * 2 * CH + CH, CH)], w_sem.at[0]).start()
        wd_copy.start()

    far = lax.rem(z + 2, 4)
    pair = far // 2
    units = ((0, 0, WIDE), (0, WIDE, WIDE), (1, far * 1024, 1024), (1, (4 * pair + 1 - far) * 1024, 1024), (1, (1 - pair) * WIDE, WIDE))
    offsets = (0, 1, -1, 2)

    def aligned(start, size):
        return pl.ds(start if isinstance(start, int) else pl.multiple_of(start, 256), size)

    def unit_columns(g, part):
        _, begin, size = units[g]
        return aligned(begin, size) if part is None else aligned(begin + part * (size // 2), size // 2)

    def xfer(g, h, idx, du, dv, part, ring, way):
        u, v = (x, y) if h == 0 else (y, x)
        bu, bv = wrap(u + du), wrap(v + dv)
        tu, tv = (wrap(u + way), v) if ring == 0 else (u, wrap(v + way))
        (bx, by), (tx, ty) = ((bu, bv), (tu, tv)) if h == 0 else ((bv, bu), (tv, tu))
        block = buf.at[units[g][0], rows(bx, by, h), unit_columns(g, part)]
        return pltpu.make_async_remote_copy(
            src_ref=block,
            dst_ref=block,
            send_sem=ag_send.at[g * 2 + h],
            recv_sem=ag_recv.at[g * 2 + h, idx],
            device_id=dev(z, tx, ty, c),
            device_id_type=MESH,
        )

    def first_full(g, h, way, sent):
        return xfer(g, h, 0 if way == 1 else 1, 0 if sent else -way, 0, None, 0, way)

    def first_relay(g, h, way, sent):
        idx, part = (2, 0) if way == 1 else (3, 1)
        return xfer(g, h, idx, -way if sent else 2, 0, part, 0, way)

    def second_full(g, h, q, way, sent):
        return xfer(g, h, 4 + 4 * q + (0 if way == 1 else 1), offsets[q], 0 if sent else -way, None, 1, way)

    def second_relay(g, h, q, way, sent):
        idx, part = (4 + 4 * q + 2, 0) if way == 1 else (4 + 4 * q + 3, 1)
        return xfer(g, h, idx, offsets[q], -way if sent else 2, part, 1, way)

    def gather(*acts):
        for g, h, what in acts:
            if what == 0:
                for way in (1, -1):
                    first_full(g, h, way, True).start()
                for way in (1, -1):
                    second_full(g, h, 0, way, True).start()
            elif what < 3:
                way, q = ((1, 2), (-1, 1))[what - 1]
                first_full(g, h, way, False).wait_recv()
                first_relay(g, h, way, True).start()
                for to in (1, -1):
                    second_full(g, h, q, to, True).start()
            elif what == 3:
                for way in (1, -1):
                    first_relay(g, h, way, False).wait_recv()
                for to in (1, -1):
                    second_full(g, h, 3, to, True).start()
            elif what < 12:
                q, way = (what - 4) // 2, 1 - 2 * (what % 2)
                second_full(g, h, q, way, False).wait_recv()
                second_relay(g, h, q, way, True).start()
            else:
                for q in range(4):
                    for way in (1, -1):
                        second_relay(g, h, q, way, False).wait_recv()

    def whole(ref, sem):
        return pltpu.make_async_copy(ref, ref, sem)

    def columns(zb, pc):
        return pl.ds(pl.multiple_of(zb * 1024 + xh * 512 + pc * BLK, BLK), BLK)

    def own_strip(zb):
        return pl.ds(pl.multiple_of(zb * BLK, BLK), BLK)

    def strips(g):
        a, begin, size = units[g]
        return [begin // 1024 + i for i in range(size // 1024)]

    def sibling_columns(g):
        for zb in strips(g):
            pltpu.make_async_remote_copy(
                src_ref=buf.at[units[g][0], :, columns(zb, 1 - c)],
                dst_ref=sib.at[units[g][0], :, own_strip(zb)],
                send_sem=sib_send.at[g],
                recv_sem=sib_recv.at[g],
                device_id=sibling,
                device_id_type=MESH,
            ).start()

    def sibling_wait(g, sem):
        a, begin, size = units[g]
        whole(sib.at[a, :, aligned(begin // 4, size // 4)], sem.at[g]).wait()

    def chunk(j):
        return pl.ds(pl.multiple_of(j * 2 * CH, 2 * CH), 2 * CH)

    pieces = ((0, 3), (3, 5), (5, 7))

    def pre_first(piece):
        j0, j1 = pieces[piece]
        if piece == 0:
            whole(wgu, w_sem.at[0]).wait()
        at = pl.ds(j0 * 2 * CH, (j1 - j0) * 2 * CH)
        ab[:, at] = times(buf[0, :, :WIDE], wgu[:WIDE, at])

    def pre_second(piece):
        j0, j1 = pieces[piece]
        at = pl.ds(j0 * 2 * CH, (j1 - j0) * 2 * CH)
        pre = ab[:, at] + times(buf[0, :, WIDE:], wgu[WIDE:, at])
        for j in range(j0, j1):
            begin = (j - j0) * 2 * CH
            gate_pre, up_pre = pre[:, begin : begin + CH], pre[:, begin + CH : begin + 2 * CH]
            sigma = jax.nn.sigmoid(gate_pre)
            swish = gate_pre * sigma
            hidden = swish * up_pre
            ab[:, chunk(j)] = jnp.concatenate([up_pre * sigma * (1.0 + gate_pre * (1.0 - sigma)), swish], axis=1)
            ht[pl.ds(j * CH, CH), pl.ds(0, TOK)] = hidden.T.astype(BF16)
        part = pl.ds(j0 * CH, (j1 - j0) * CH)
        pltpu.make_async_remote_copy(
            src_ref=ht.at[part, pl.ds(0, TOK)],
            dst_ref=ht.at[part, pl.ds(TOK, TOK)],
            send_sem=ht_send.at[0],
            recv_sem=ht_recv.at[0],
            device_id=sibling,
            device_id_type=MESH,
        ).start()

    def first_hidden_grad(piece):
        at, half = ((pl.ds(0, 512), pl.ds(512, 384))[piece], aligned(pair * WIDE, WIDE))
        if piece == 0:
            wd_copy.wait()
        hga[:, at] = times_transposed(buf[1, :, half], wd[at, half])

    def delta_size(i):
        return min(2, NCH - 2 * i) * CH

    def delta_chunk(i):
        at, half = pl.ds(i * 2 * CH, delta_size(i)), aligned((1 - pair) * WIDE, WIDE)
        hg = hga[:, at] + times_transposed(buf[1, :, half], wd[at, half])
        for w in range(delta_size(i) // CH):
            part = hg[:, w * CH : (w + 1) * CH]
            to = chunk(2 * i + w)
            gu[pl.ds(0, TOK), to] = (jnp.concatenate([part, part], axis=1) * ab[:, to]).astype(BF16)
        delta_copy(i).start()

    def delta_columns(i):
        return pl.ds(i * 4 * CH, 2 * delta_size(i))

    def delta_copy(i):
        return pltpu.make_async_remote_copy(
            src_ref=gu.at[pl.ds(0, TOK), delta_columns(i)],
            dst_ref=gu.at[pl.ds(TOK, TOK), delta_columns(i)],
            send_sem=gu_send.at[i],
            recv_sem=gu_recv.at[i],
            device_id=sibling,
            device_id_type=MESH,
        )

    def transposed_x():
        sibling_wait(0, sib_recv)
        sibling_wait(1, sib_recv)

        @pl.loop(0, 4)
        def _(k):
            zb = lax.rem(z + k, 4)
            xt[k, :, pl.ds(0, TOK)] = buf[0, :, columns(zb, c)].T
            xt[k, :, pl.ds(TOK, TOK)] = sib[0, :, own_strip(zb)].T

    def down_part(k):
        zb = lax.rem(z + k, 4)
        total = times(ht[:, pl.ds(0, TOK)], buf[1, :, columns(zb, c)])
        total += times(ht[:, pl.ds(TOK, TOK)], sib[1, :, own_strip(zb)])
        dpart[k] = total.astype(BF16)

    def gu_part(i, k):
        gpart[k, :, delta_columns(i)] = times(xt[k], gu[:, delta_columns(i)]).astype(BF16)

    sums = [(dpart, r1d, r2d, pl.ds(0, BLK))] + [(gpart, r1g, r2g, delta_columns(i)) for i in range(4)]

    def z_side(side):
        return dev(wrap(z + 1 - 2 * side), x, y, c)

    def half_of(i, side):
        size = sums[i][0].shape[1] // 2
        return pl.ds(side * size if isinstance(side, int) else pl.multiple_of(side * size, size), size)

    def first(i, side):
        part, received, _, cols = sums[i]
        return pltpu.make_async_remote_copy(
            src_ref=part.at[2, half_of(i, side), cols],
            dst_ref=received.at[side, :, cols],
            send_sem=s1_send.at[i, side],
            recv_sem=s1_recv.at[i, side],
            device_id=z_side(side),
            device_id_type=MESH,
        )

    def second(i, side):
        part, _, received, cols = sums[i]
        return pltpu.make_async_remote_copy(
            src_ref=part.at[1 + 2 * side, :, cols],
            dst_ref=received.at[side, :, cols],
            send_sem=s2_send.at[i, side],
            recv_sem=s2_recv.at[i, side],
            device_id=z_side(side),
            device_id_type=MESH,
        )

    def add_first(i, side):
        part, received, _, cols = sums[i]
        first(i, side).wait_recv()
        k, half = 1 + 2 * side, half_of(i, side)
        part[k, half, cols] = (part[k, half, cols].astype(F32) + received[side, :, cols].astype(F32)).astype(BF16)
        second(i, side).start()

    def add_second(i):
        part, _, received, cols = sums[i]
        for side in range(2):
            second(i, side).wait_recv()
        total = part[0, :, cols].astype(F32) + received[0, :, cols].astype(F32)
        return total + received[1, :, cols].astype(F32)

    side_a = 1 - lax.rem(z, 2)
    side_b = 1 - side_a

    def down_far():
        whole(ht.at[:, pl.ds(TOK, TOK)], ht_recv.at[0]).wait()
        sibling_wait(2, sib_recv)
        down_part(2)
        first(0, 0).start()
        first(0, 1).start()

    def down_near():
        sibling_wait(3, sib_recv)
        down_part(1 + 2 * side_a)

    def gu_far(i):
        delta_copy(i).wait_recv()
        gu_part(i, 2)
        first(1 + i, 0).start()
        first(1 + i, 1).start()

    def gu_near(i):
        for side in range(2):
            gu_part(i, 1 + 2 * side)
        for side in range(2):
            add_first(1 + i, side)

    def dx_rows(s):
        return pl.ds(pl.multiple_of(s * ROWS, ROWS), ROWS)

    def dx_copy(o, half):
        to = lax.rem(t + o, 8)
        at = pl.ds(half * WIDE, WIDE)
        return pltpu.make_async_remote_copy(
            src_ref=dxs.at[dx_rows(to), at],
            dst_ref=dxr.at[dx_rows(t), at],
            send_sem=dx_send.at[half, o],
            recv_sem=dx_recv.at[half, o],
            device_id=(dp, to),
            device_id_type=MESH,
        )

    def dx_part(half):
        mine = gu[pl.ds(pl.multiple_of(xh * 256, 256), 256), :]
        for n in range(2):
            strip = pl.ds(half * WIDE + n * 1024, 1024)
            dxs[:, strip] = times_transposed(mine, wgu[strip, :]).astype(BF16)

        for o in range(1, 8):
            dx_copy(o, half).start()

    gather((0, 0, 0), (0, 1, 0), (1, 0, 0), (1, 1, 0))
    load_weights()
    gather((0, 0, 1), (0, 0, 2), (0, 0, 4), (0, 0, 5), (0, 1, 4), (0, 1, 5), (0, 1, 1), (0, 1, 2), (1, 0, 2))
    gather((1, 0, 1), (1, 1, 5), (1, 1, 4), (1, 0, 5), (1, 0, 4), (1, 1, 2), (1, 1, 1), (0, 0, 3), (0, 1, 3))
    gather((2, 1, 0), (1, 0, 3), (0, 1, 8), (0, 1, 6), (0, 1, 9), (0, 1, 7), (0, 0, 9), (0, 0, 8), (0, 0, 7))
    gather((0, 0, 6), (1, 1, 3), (2, 1, 5), (2, 1, 4), (2, 0, 0), (1, 0, 6), (1, 0, 7), (2, 1, 1), (2, 1, 2))
    gather((1, 0, 8), (1, 0, 9), (1, 1, 7), (1, 1, 9), (1, 1, 6), (1, 1, 8), (3, 0, 0), (0, 1, 11), (0, 1, 10))
    gather((4, 0, 0), (0, 0, 11), (0, 0, 10), (3, 1, 0), (2, 1, 3), (1, 0, 11), (1, 0, 10), (2, 0, 1), (2, 0, 2))
    gather((2, 0, 5), (2, 0, 4), (4, 1, 0), (3, 0, 4), (3, 0, 5), (2, 1, 8), (2, 1, 6), (2, 1, 9), (2, 1, 7))
    gather((0, 0, 12), (3, 0, 1), (3, 0, 2), (0, 1, 12))
    sibling_columns(0)
    pre_first(0)
    gather((1, 1, 10), (1, 1, 11), (1, 0, 12), (2, 0, 3), (2, 1, 11), (2, 1, 10), (2, 0, 9), (2, 0, 8), (3, 1, 1))
    gather((3, 1, 2), (2, 0, 7), (2, 0, 6), (3, 1, 5), (3, 1, 4))
    pre_first(1)
    gather((3, 0, 3), (4, 0, 4), (4, 0, 5), (4, 0, 1), (4, 0, 2), (4, 1, 4), (4, 1, 5))
    pre_first(2)
    gather((3, 0, 8), (3, 0, 9), (3, 0, 6), (3, 0, 7), (4, 1, 1), (4, 1, 2), (2, 1, 12), (3, 1, 3), (1, 1, 12))
    sibling_columns(1)
    pre_second(0)
    gather((2, 0, 11), (2, 0, 10), (3, 1, 8), (3, 1, 9), (3, 1, 6), (3, 1, 7), (4, 0, 3))
    pre_second(1)
    gather((3, 0, 11), (3, 0, 10), (3, 1, 10), (3, 1, 11), (4, 1, 3))
    pre_second(2)
    gather((4, 0, 8), (2, 0, 12))
    sibling_columns(2)
    gather((4, 0, 9), (4, 0, 6), (4, 0, 7), (4, 1, 8), (4, 1, 6), (4, 1, 9), (4, 1, 7))
    transposed_x()
    gather((3, 0, 12), (3, 1, 12))
    sibling_columns(3)
    first_hidden_grad(0)
    gather((4, 0, 10), (4, 0, 11), (4, 1, 11), (4, 1, 10))
    down_far()
    down_near()
    first_hidden_grad(1)
    gather((4, 0, 12), (4, 1, 12))
    sibling_columns(4)
    delta_chunk(0)
    delta_chunk(1)
    add_first(0, side_a)
    gu_far(0)
    delta_chunk(2)
    gu_far(1)
    delta_chunk(3)
    sibling_wait(4, sib_recv)
    down_part(1 + 2 * side_b)
    add_first(0, side_b)
    gu_far(2)
    gu_far(3)
    dx_part(0)
    gu_near(0)
    dx_part(1)
    gu_near(1)
    gu_near(2)
    gu_near(3)
    down_part(0)
    for i in range(4):
        gu_part(i, 0)

    for i in range(5):
        for side in range(2):
            first(i, side).wait_send()
    outs = [
        pltpu.make_async_copy(dpart.at[2], dg_out, out_sem.at[0]),
        pltpu.make_async_copy(dxs.at[dx_rows(t), :], dx_out, out_sem.at[1]),
        pltpu.make_async_copy(gfin, gg_out, out_sem.at[2]),
        pltpu.make_async_copy(ufin, ug_out, out_sem.at[3]),
    ]
    dpart[2] = add_second(0).astype(BF16)
    outs[0].start()

    def grads(i):
        total = add_second(1 + i)
        for w in range(delta_size(i) // CH):
            at = pl.ds((2 * i + w) * CH, CH)
            gfin[:, at] = total[:, 2 * w * CH : (2 * w + 1) * CH].astype(BF16)
            ufin[:, at] = total[:, (2 * w + 1) * CH : (2 * w + 2) * CH].astype(BF16)

    grads(0)
    grads(1)
    for half in range(2):
        for o in range(1, 8):
            dx_copy(o, half).wait_recv()
    total = dxs[dx_rows(t), :].astype(F32)
    for o in range(1, 8):
        total += dxr[dx_rows(lax.rem(t + o, 8)), :].astype(F32)
    dxs[dx_rows(t), :] = total.astype(BF16)
    outs[1].start()
    grads(2)
    grads(3)
    outs[2].start()
    outs[3].start()

    for g, (_, _, size) in enumerate(units):
        for h in range(2):
            whole(buf.at[0, pl.ds(0, 15 * HALF), pl.ds(0, size)], ag_send.at[g * 2 + h]).wait()
        sibling_wait(g, sib_send)
    whole(ht.at[:, pl.ds(0, TOK)], ht_send.at[0]).wait()
    for i in range(4):
        delta_copy(i).wait_send()
    for i in range(5):
        for side in range(2):
            second(i, side).wait_send()
    for half in range(2):
        for o in range(1, 8):
            dx_copy(o, half).wait_send()
    for copy in outs:
        copy.wait()


def hand_on(*refs):
    for given, result in zip(refs[:4], refs[4:]):
        result[...] = given[...]


def per_device(layer_input, output_grad, gate_weight, up_weight, down_weight):
    dma = pltpu.SemaphoreType.DMA
    vmem = pltpu.VMEM
    results = (
        jax.ShapeDtypeStruct((ROWS, D), BF16),
        jax.ShapeDtypeStruct((BLK, F), BF16),
        jax.ShapeDtypeStruct((BLK, F), BF16),
        jax.ShapeDtypeStruct((F, BLK), BF16),
    )
    found = pl.pallas_call(
        kernel,
        out_shape=results,
        in_specs=[pl.BlockSpec(memory_space=pl.ANY)] * 5,
        out_specs=[pl.BlockSpec(memory_space=pl.ANY)] * 4,
        scratch_shapes=[
            vmem((2, TOK, D), BF16),
            vmem((2, TOK, 4 * BLK), BF16),
            vmem((D, 2 * F), BF16),
            vmem((F, D), BF16),
            vmem((TOK, 2 * F), F32),
            vmem((TOK, F), F32),
            vmem((2 * TOK, 2 * F), BF16),
            vmem((F, 2 * TOK), BF16),
            vmem((4, BLK, 2 * TOK), BF16),
            vmem((4, F, BLK), BF16),
            vmem((4, BLK, 2 * F), BF16),
            vmem((2, F // 2, BLK), BF16),
            vmem((2, BLK // 2, 2 * F), BF16),
            vmem((2, F, BLK), BF16),
            vmem((2, BLK, 2 * F), BF16),
            vmem((8 * ROWS, D), BF16),
            vmem((8 * ROWS, D), BF16),
            vmem((BLK, F), BF16),
            vmem((BLK, F), BF16),
            dma((10,)),
            dma((10, 20)),
            dma((2,)),
            dma((2,)),
            dma((5,)),
            dma((5,)),
            dma((1,)),
            dma((1,)),
            dma((4,)),
            dma((4,)),
            dma((5, 2)),
            dma((5, 2)),
            dma((5, 2)),
            dma((5, 2)),
            dma((2, 8)),
            dma((2, 8)),
            dma((4,)),
        ],
        compiler_params=pltpu.CompilerParams(
            collective_id=0, has_side_effects=True, vmem_limit_bytes=63 * 1024 * 1024
        ),
        cost_estimate=pl.CostEstimate(flops=21 * 10**9, bytes_accessed=26 * 10**6, transcendentals=10**6),
    )(layer_input, output_grad, gate_weight, up_weight, down_weight)
    return pl.pallas_call(
        hand_on,
        out_shape=results,
        in_specs=[pl.BlockSpec(memory_space=pltpu.VMEM)] * 4,
        out_specs=[pl.BlockSpec(memory_space=pltpu.VMEM)] * 4,
        cost_estimate=pl.CostEstimate(flops=0, bytes_accessed=4 * 10**6, transcendentals=0),
    )(*found)


def solution(mesh):
    placed = (
        P(("dp", "tensor"), None),
        P(("dp", "tensor"), None),
        P(None, "tensor"),
        P(None, "tensor"),
        P("tensor", None),
    )
    return jax.shard_map(
        per_device,
        mesh=mesh,
        in_specs=placed,
        out_specs=(
            P(("dp", "tensor"), None),
            P("dp", "tensor"),
            P("dp", "tensor"),
            P("tensor", "dp"),
        ),
        check_vma=False,
    )
```

```python
import jax
import jax.numpy as jnp
from jax import lax
from jax.experimental import pallas as pl
from jax.experimental.pallas import tpu as pltpu
from jax.sharding import PartitionSpec as P

MESH = pl.DeviceIdType.MESH
BF16, F32 = jnp.bfloat16, jnp.float32

D = 4096
F = 896
ROWS = 32
TOK = 512
HALF = 16
BLK = 256
CH = 128
NCH = F // CH
WIDE = D // 2


def times_transposed(left, right):
    return lax.dot_general(left, right, (((1,), (1,)), ((), ())), preferred_element_type=F32)


def times(left, right):
    return jnp.dot(left, right, preferred_element_type=F32)


def kernel(
    x_hbm, dy_hbm, gw_hbm, uw_hbm, dw_hbm,
    dx_out, gg_out, ug_out, dg_out,
    buf, sib, wgu, wd, ab, hga, gu, ht, xt, dpart, gpart, r1d, r1g, r2d, r2g, dxs, dxr, gfin, ufin,
    ag_send, ag_recv, w_sem, own_sem, sib_send, sib_recv, ht_send, ht_recv, gu_send, gu_recv,
    s1_send, s1_recv, s2_send, s2_recv, dx_send, dx_recv, out_sem,
):
    dp, t = lax.axis_index("dp"), lax.axis_index("tensor")
    c, xh, z = lax.rem(dp, 2), lax.rem(dp // 2, 2), dp // 4
    y, xl = t // 2, lax.rem(t, 2)
    x = 2 * xh + xl

    def wrap(v):
        return lax.rem(v + 4, 4)

    def dev(pz, px, py, pc):
        return ((pz * 2 + px // 2) * 2 + pc, py * 2 + lax.rem(px, 2))

    sibling = dev(z, x, y, 1 - c)
    z_next, z_prev = dev(wrap(z + 1), x, y, c), dev(wrap(z - 1), x, y, c)

    barrier = pltpu.get_barrier_semaphore()
    greeted = [(dp, lax.rem(t + o, 8)) for o in range(1, 8)]
    greeted += [dev(z, wrap(x + 2 * xl - 1), y, c), z_next, z_prev, sibling]
    for other in greeted:
        pl.semaphore_signal(barrier, inc=1, device_id=other, device_id_type=MESH)

    def rows(px, py, h):
        slot = (px // 2) * 8 + py * 2 + lax.rem(px, 2)
        return pl.ds(pl.multiple_of(slot * ROWS + h * HALF, HALF), HALF)

    own = pl.ds(pl.multiple_of((xh * 8 + t) * ROWS, ROWS), ROWS)
    own_copies = [
        pltpu.make_async_copy(src, buf.at[a, own, :], own_sem.at[a]) for a, src in enumerate((x_hbm, dy_hbm))
    ]
    for copy in own_copies:
        copy.start()
    for copy in own_copies:
        copy.wait()
    pl.semaphore_wait(barrier, len(greeted))

    wd_copy = pltpu.make_async_copy(dw_hbm, wd, w_sem.at[1])

    def load_weights():
        for j in range(NCH):
            part = pl.ds(j * CH, CH)
            pltpu.make_async_copy(gw_hbm.at[:, part], wgu.at[:, pl.ds(j * 2 * CH, CH)], w_sem.at[0]).start()
            pltpu.make_async_copy(uw_hbm.at[:, part], wgu.at[:, pl.ds(j * 2 * CH + CH, CH)], w_sem.at[0]).start()
        wd_copy.start()

    far = lax.rem(z + 2, 4)
    pair = far // 2
    units = ((0, 0, WIDE), (0, WIDE, WIDE), (1, far * 1024, 1024), (1, (4 * pair + 1 - far) * 1024, 1024), (1, (1 - pair) * WIDE, WIDE))
    offsets = (0, 1, -1, 2)

    def aligned(start, size):
        return pl.ds(start if isinstance(start, int) else pl.multiple_of(start, 256), size)

    def unit_columns(g, part):
        _, begin, size = units[g]
        return aligned(begin, size) if part is None else aligned(begin + part * (size // 2), size // 2)

    def xfer(g, h, idx, du, dv, part, ring, way):
        u, v = (x, y) if h == 0 else (y, x)
        bu, bv = wrap(u + du), wrap(v + dv)
        tu, tv = (wrap(u + way), v) if ring == 0 else (u, wrap(v + way))
        (bx, by), (tx, ty) = ((bu, bv), (tu, tv)) if h == 0 else ((bv, bu), (tv, tu))
        block = buf.at[units[g][0], rows(bx, by, h), unit_columns(g, part)]
        return pltpu.make_async_remote_copy(
            src_ref=block,
            dst_ref=block,
            send_sem=ag_send.at[g * 2 + h],
            recv_sem=ag_recv.at[g * 2 + h, idx],
            device_id=dev(z, tx, ty, c),
            device_id_type=MESH,
        )

    def first_full(g, h, way, sent):
        return xfer(g, h, 0 if way == 1 else 1, 0 if sent else -way, 0, None, 0, way)

    def first_relay(g, h, way, sent):
        idx, part = (2, 0) if way == 1 else (3, 1)
        return xfer(g, h, idx, -way if sent else 2, 0, part, 0, way)

    def second_full(g, h, q, way, sent):
        return xfer(g, h, 4 + 4 * q + (0 if way == 1 else 1), offsets[q], 0 if sent else -way, None, 1, way)

    def second_relay(g, h, q, way, sent):
        idx, part = (4 + 4 * q + 2, 0) if way == 1 else (4 + 4 * q + 3, 1)
        return xfer(g, h, idx, offsets[q], -way if sent else 2, part, 1, way)

    def gather(*acts):
        for g, h, what in acts:
            if what == 0:
                for way in (1, -1):
                    first_full(g, h, way, True).start()
                for way in (1, -1):
                    second_full(g, h, 0, way, True).start()
            elif what < 3:
                way, q = ((1, 2), (-1, 1))[what - 1]
                first_full(g, h, way, False).wait_recv()
                first_relay(g, h, way, True).start()
                for to in (1, -1):
                    second_full(g, h, q, to, True).start()
            elif what == 3:
                for way in (1, -1):
                    first_relay(g, h, way, False).wait_recv()
                for to in (1, -1):
                    second_full(g, h, 3, to, True).start()
            elif what < 12:
                q, way = (what - 4) // 2, 1 - 2 * (what % 2)
                second_full(g, h, q, way, False).wait_recv()
                second_relay(g, h, q, way, True).start()
            else:
                for q in range(4):
                    for way in (1, -1):
                        second_relay(g, h, q, way, False).wait_recv()

    def whole(ref, sem):
        return pltpu.make_async_copy(ref, ref, sem)

    def columns(zb, pc):
        return pl.ds(pl.multiple_of(zb * 1024 + xh * 512 + pc * BLK, BLK), BLK)

    def own_strip(zb):
        return pl.ds(pl.multiple_of(zb * BLK, BLK), BLK)

    def strips(g):
        a, begin, size = units[g]
        return [begin // 1024 + i for i in range(size // 1024)]

    def sibling_columns(g):
        for zb in strips(g):
            pltpu.make_async_remote_copy(
                src_ref=buf.at[units[g][0], :, columns(zb, 1 - c)],
                dst_ref=sib.at[units[g][0], :, own_strip(zb)],
                send_sem=sib_send.at[g],
                recv_sem=sib_recv.at[g],
                device_id=sibling,
                device_id_type=MESH,
            ).start()

    def sibling_wait(g, sem):
        a, begin, size = units[g]
        whole(sib.at[a, :, aligned(begin // 4, size // 4)], sem.at[g]).wait()

    def chunk(j):
        return pl.ds(pl.multiple_of(j * 2 * CH, 2 * CH), 2 * CH)

    pieces = ((0, 3), (3, 5), (5, 7))

    def pre_first(piece):
        j0, j1 = pieces[piece]
        if piece == 0:
            whole(wgu, w_sem.at[0]).wait()
        for j in range(j0, j1):
            ab[:, chunk(j)] = times(buf[0, :, :WIDE], wgu[:WIDE, chunk(j)])

    def pre_second(piece):
        j0, j1 = pieces[piece]
        for j in range(j0, j1):
            pre = ab[:, chunk(j)] + times(buf[0, :, WIDE:], wgu[WIDE:, chunk(j)])
            gate_pre, up_pre = pre[:, :CH], pre[:, CH:]
            sigma = jax.nn.sigmoid(gate_pre)
            swish = gate_pre * sigma
            hidden = swish * up_pre
            ab[:, chunk(j)] = jnp.concatenate([up_pre * sigma * (1.0 + gate_pre * (1.0 - sigma)), swish], axis=1)
            ht[pl.ds(j * CH, CH), pl.ds(0, TOK)] = hidden.T.astype(BF16)
        part = pl.ds(j0 * CH, (j1 - j0) * CH)
        pltpu.make_async_remote_copy(
            src_ref=ht.at[part, pl.ds(0, TOK)],
            dst_ref=ht.at[part, pl.ds(TOK, TOK)],
            send_sem=ht_send.at[0],
            recv_sem=ht_recv.at[0],
            device_id=sibling,
            device_id_type=MESH,
        ).start()

    def first_hidden_grad(piece):
        at, half = ((pl.ds(0, 512), pl.ds(512, 384))[piece], aligned(pair * WIDE, WIDE))
        if piece == 0:
            wd_copy.wait()
        hga[:, at] = times_transposed(buf[1, :, half], wd[at, half])

    def delta_size(i):
        return min(2, NCH - 2 * i) * CH

    def delta_chunk(i):
        at, half = pl.ds(i * 2 * CH, delta_size(i)), aligned((1 - pair) * WIDE, WIDE)
        hg = hga[:, at] + times_transposed(buf[1, :, half], wd[at, half])
        for w in range(delta_size(i) // CH):
            part = hg[:, w * CH : (w + 1) * CH]
            to = chunk(2 * i + w)
            gu[pl.ds(0, TOK), to] = (jnp.concatenate([part, part], axis=1) * ab[:, to]).astype(BF16)
        delta_copy(i).start()

    def delta_columns(i):
        return pl.ds(i * 4 * CH, 2 * delta_size(i))

    def delta_copy(i):
        return pltpu.make_async_remote_copy(
            src_ref=gu.at[pl.ds(0, TOK), delta_columns(i)],
            dst_ref=gu.at[pl.ds(TOK, TOK), delta_columns(i)],
            send_sem=gu_send.at[i],
            recv_sem=gu_recv.at[i],
            device_id=sibling,
            device_id_type=MESH,
        )

    def transposed_x():
        sibling_wait(0, sib_recv)
        sibling_wait(1, sib_recv)

        @pl.loop(0, 4)
        def _(k):
            zb = lax.rem(z + k, 4)
            xt[k, :, pl.ds(0, TOK)] = buf[0, :, columns(zb, c)].T
            xt[k, :, pl.ds(TOK, TOK)] = sib[0, :, own_strip(zb)].T

    def down_part(k):
        zb = lax.rem(z + k, 4)
        total = times(ht[:, pl.ds(0, TOK)], buf[1, :, columns(zb, c)])
        total += times(ht[:, pl.ds(TOK, TOK)], sib[1, :, own_strip(zb)])
        dpart[k] = total.astype(BF16)

    def gu_part(i, k):
        gpart[k, :, delta_columns(i)] = times(xt[k], gu[:, delta_columns(i)]).astype(BF16)

    sums = [(dpart, r1d, r2d, pl.ds(0, BLK))] + [(gpart, r1g, r2g, delta_columns(i)) for i in range(4)]

    def z_side(side):
        return dev(wrap(z + 1 - 2 * side), x, y, c)

    def half_of(i, side):
        size = sums[i][0].shape[1] // 2
        return pl.ds(side * size if isinstance(side, int) else pl.multiple_of(side * size, size), size)

    def first(i, side):
        part, received, _, cols = sums[i]
        return pltpu.make_async_remote_copy(
            src_ref=part.at[2, half_of(i, side), cols],
            dst_ref=received.at[side, :, cols],
            send_sem=s1_send.at[i, side],
            recv_sem=s1_recv.at[i, side],
            device_id=z_side(side),
            device_id_type=MESH,
        )

    def second(i, side):
        part, _, received, cols = sums[i]
        return pltpu.make_async_remote_copy(
            src_ref=part.at[1 + 2 * side, :, cols],
            dst_ref=received.at[side, :, cols],
            send_sem=s2_send.at[i, side],
            recv_sem=s2_recv.at[i, side],
            device_id=z_side(side),
            device_id_type=MESH,
        )

    def add_first(i, side):
        part, received, _, cols = sums[i]
        first(i, side).wait_recv()
        k, half = 1 + 2 * side, half_of(i, side)
        part[k, half, cols] = (part[k, half, cols].astype(F32) + received[side, :, cols].astype(F32)).astype(BF16)
        second(i, side).start()

    def add_second(i):
        part, _, received, cols = sums[i]
        for side in range(2):
            second(i, side).wait_recv()
        total = part[0, :, cols].astype(F32) + received[0, :, cols].astype(F32)
        return total + received[1, :, cols].astype(F32)

    side_a = 1 - lax.rem(z, 2)
    side_b = 1 - side_a

    def down_far():
        whole(ht.at[:, pl.ds(TOK, TOK)], ht_recv.at[0]).wait()
        sibling_wait(2, sib_recv)
        down_part(2)
        first(0, 0).start()
        first(0, 1).start()

    def down_near():
        sibling_wait(3, sib_recv)
        down_part(1 + 2 * side_a)

    def gu_far(i):
        delta_copy(i).wait_recv()
        gu_part(i, 2)
        first(1 + i, 0).start()
        first(1 + i, 1).start()

    def gu_near(i):
        for side in range(2):
            gu_part(i, 1 + 2 * side)
        for side in range(2):
            add_first(1 + i, side)

    def dx_rows(s):
        return pl.ds(pl.multiple_of(s * ROWS, ROWS), ROWS)

    def dx_copy(o, half):
        to = lax.rem(t + o, 8)
        at = pl.ds(half * WIDE, WIDE)
        return pltpu.make_async_remote_copy(
            src_ref=dxs.at[dx_rows(to), at],
            dst_ref=dxr.at[dx_rows(t), at],
            send_sem=dx_send.at[half, o],
            recv_sem=dx_recv.at[half, o],
            device_id=(dp, to),
            device_id_type=MESH,
        )

    def dx_part(half):
        mine = gu[pl.ds(pl.multiple_of(xh * 256, 256), 256), :]
        for n in range(2):
            strip = pl.ds(half * WIDE + n * 1024, 1024)
            dxs[:, strip] = times_transposed(mine, wgu[strip, :]).astype(BF16)

        for o in range(1, 8):
            dx_copy(o, half).start()

    gather((0, 0, 0), (0, 1, 0), (1, 0, 0), (1, 1, 0))
    load_weights()
    gather((0, 0, 1), (0, 0, 2), (0, 0, 4), (0, 0, 5), (0, 1, 4), (0, 1, 5), (0, 1, 1), (0, 1, 2), (1, 0, 2))
    gather((1, 0, 1), (1, 1, 5), (1, 1, 4), (1, 0, 5), (1, 0, 4), (1, 1, 2), (1, 1, 1), (0, 0, 3), (0, 1, 3))
    gather((2, 1, 0), (1, 0, 3), (0, 1, 8), (0, 1, 6), (0, 1, 9), (0, 1, 7), (0, 0, 9), (0, 0, 8), (0, 0, 7))
    gather((0, 0, 6), (1, 1, 3), (2, 1, 5), (2, 1, 4), (2, 0, 0), (1, 0, 6), (1, 0, 7), (2, 1, 1), (2, 1, 2))
    gather((1, 0, 8), (1, 0, 9), (1, 1, 7), (1, 1, 9), (1, 1, 6), (1, 1, 8), (3, 0, 0), (0, 1, 11), (0, 1, 10))
    gather((4, 0, 0), (0, 0, 11), (0, 0, 10), (3, 1, 0), (2, 1, 3), (1, 0, 11), (1, 0, 10), (2, 0, 1), (2, 0, 2))
    gather((2, 0, 5), (2, 0, 4), (4, 1, 0), (3, 0, 4), (3, 0, 5), (2, 1, 8), (2, 1, 6), (2, 1, 9), (2, 1, 7))
    gather((0, 0, 12), (3, 0, 1), (3, 0, 2), (0, 1, 12))
    sibling_columns(0)
    pre_first(0)
    gather((1, 1, 10), (1, 1, 11), (1, 0, 12), (2, 0, 3), (2, 1, 11), (2, 1, 10), (2, 0, 9), (2, 0, 8), (3, 1, 1))
    gather((3, 1, 2), (2, 0, 7), (2, 0, 6), (3, 1, 5), (3, 1, 4))
    pre_first(1)
    gather((3, 0, 3), (4, 0, 4), (4, 0, 5), (4, 0, 1), (4, 0, 2), (4, 1, 4), (4, 1, 5))
    pre_first(2)
    gather((3, 0, 8), (3, 0, 9), (3, 0, 6), (3, 0, 7), (4, 1, 1), (4, 1, 2), (2, 1, 12), (3, 1, 3), (1, 1, 12))
    sibling_columns(1)
    pre_second(0)
    gather((2, 0, 11), (2, 0, 10), (3, 1, 8), (3, 1, 9), (3, 1, 6), (3, 1, 7), (4, 0, 3))
    pre_second(1)
    gather((3, 0, 11), (3, 0, 10), (3, 1, 10), (3, 1, 11), (4, 1, 3))
    pre_second(2)
    gather((4, 0, 8), (2, 0, 12))
    sibling_columns(2)
    gather((4, 0, 9), (4, 0, 6), (4, 0, 7), (4, 1, 8), (4, 1, 6), (4, 1, 9), (4, 1, 7))
    transposed_x()
    gather((3, 0, 12), (3, 1, 12))
    sibling_columns(3)
    first_hidden_grad(0)
    gather((4, 0, 10), (4, 0, 11), (4, 1, 11), (4, 1, 10))
    down_far()
    down_near()
    first_hidden_grad(1)
    gather((4, 0, 12), (4, 1, 12))
    sibling_columns(4)
    delta_chunk(0)
    delta_chunk(1)
    add_first(0, side_a)
    gu_far(0)
    delta_chunk(2)
    gu_far(1)
    delta_chunk(3)
    sibling_wait(4, sib_recv)
    down_part(1 + 2 * side_b)
    add_first(0, side_b)
    gu_far(2)
    gu_far(3)
    dx_part(0)
    gu_near(0)
    dx_part(1)
    gu_near(1)
    gu_near(2)
    gu_near(3)
    down_part(0)
    for i in range(4):
        gu_part(i, 0)

    for i in range(5):
        for side in range(2):
            first(i, side).wait_send()
    outs = [
        pltpu.make_async_copy(dpart.at[2], dg_out, out_sem.at[0]),
        pltpu.make_async_copy(dxs.at[dx_rows(t), :], dx_out, out_sem.at[1]),
        pltpu.make_async_copy(gfin, gg_out, out_sem.at[2]),
        pltpu.make_async_copy(ufin, ug_out, out_sem.at[3]),
    ]
    dpart[2] = add_second(0).astype(BF16)
    outs[0].start()

    def grads(i):
        total = add_second(1 + i)
        for w in range(delta_size(i) // CH):
            at = pl.ds((2 * i + w) * CH, CH)
            gfin[:, at] = total[:, 2 * w * CH : (2 * w + 1) * CH].astype(BF16)
            ufin[:, at] = total[:, (2 * w + 1) * CH : (2 * w + 2) * CH].astype(BF16)

    grads(0)
    grads(1)
    for half in range(2):
        for o in range(1, 8):
            dx_copy(o, half).wait_recv()
    total = dxs[dx_rows(t), :].astype(F32)
    for o in range(1, 8):
        total += dxr[dx_rows(lax.rem(t + o, 8)), :].astype(F32)
    dxs[dx_rows(t), :] = total.astype(BF16)
    outs[1].start()
    grads(2)
    grads(3)
    outs[2].start()
    outs[3].start()

    for g, (_, _, size) in enumerate(units):
        for h in range(2):
            whole(buf.at[0, pl.ds(0, 15 * HALF), pl.ds(0, size)], ag_send.at[g * 2 + h]).wait()
        sibling_wait(g, sib_send)
    whole(ht.at[:, pl.ds(0, TOK)], ht_send.at[0]).wait()
    for i in range(4):
        delta_copy(i).wait_send()
    for i in range(5):
        for side in range(2):
            second(i, side).wait_send()
    for half in range(2):
        for o in range(1, 8):
            dx_copy(o, half).wait_send()
    for copy in outs:
        copy.wait()


def hand_on(*refs):
    for given, result in zip(refs[:4], refs[4:]):
        result[...] = given[...]


def per_device(layer_input, output_grad, gate_weight, up_weight, down_weight):
    dma = pltpu.SemaphoreType.DMA
    vmem = pltpu.VMEM
    results = (
        jax.ShapeDtypeStruct((ROWS, D), BF16),
        jax.ShapeDtypeStruct((BLK, F), BF16),
        jax.ShapeDtypeStruct((BLK, F), BF16),
        jax.ShapeDtypeStruct((F, BLK), BF16),
    )
    found = pl.pallas_call(
        kernel,
        out_shape=results,
        in_specs=[pl.BlockSpec(memory_space=pl.ANY)] * 5,
        out_specs=[pl.BlockSpec(memory_space=pl.ANY)] * 4,
        scratch_shapes=[
            vmem((2, TOK, D), BF16),
            vmem((2, TOK, 4 * BLK), BF16),
            vmem((D, 2 * F), BF16),
            vmem((F, D), BF16),
            vmem((TOK, 2 * F), F32),
            vmem((TOK, F), F32),
            vmem((2 * TOK, 2 * F), BF16),
            vmem((F, 2 * TOK), BF16),
            vmem((4, BLK, 2 * TOK), BF16),
            vmem((4, F, BLK), BF16),
            vmem((4, BLK, 2 * F), BF16),
            vmem((2, F // 2, BLK), BF16),
            vmem((2, BLK // 2, 2 * F), BF16),
            vmem((2, F, BLK), BF16),
            vmem((2, BLK, 2 * F), BF16),
            vmem((8 * ROWS, D), BF16),
            vmem((8 * ROWS, D), BF16),
            vmem((BLK, F), BF16),
            vmem((BLK, F), BF16),
            dma((10,)),
            dma((10, 20)),
            dma((2,)),
            dma((2,)),
            dma((5,)),
            dma((5,)),
            dma((1,)),
            dma((1,)),
            dma((4,)),
            dma((4,)),
            dma((5, 2)),
            dma((5, 2)),
            dma((5, 2)),
            dma((5, 2)),
            dma((2, 8)),
            dma((2, 8)),
            dma((4,)),
        ],
        compiler_params=pltpu.CompilerParams(
            collective_id=0, has_side_effects=True, vmem_limit_bytes=63 * 1024 * 1024
        ),
        cost_estimate=pl.CostEstimate(flops=21 * 10**9, bytes_accessed=26 * 10**6, transcendentals=10**6),
    )(layer_input, output_grad, gate_weight, up_weight, down_weight)
    return pl.pallas_call(
        hand_on,
        out_shape=results,
        in_specs=[pl.BlockSpec(memory_space=pltpu.VMEM)] * 4,
        out_specs=[pl.BlockSpec(memory_space=pltpu.VMEM)] * 4,
        cost_estimate=pl.CostEstimate(flops=0, bytes_accessed=4 * 10**6, transcendentals=0),
    )(*found)


def solution(mesh):
    placed = (
        P(("dp", "tensor"), None),
        P(("dp", "tensor"), None),
        P(None, "tensor"),
        P(None, "tensor"),
        P("tensor", None),
    )
    return jax.shard_map(
        per_device,
        mesh=mesh,
        in_specs=placed,
        out_specs=(
            P(("dp", "tensor"), None),
            P("dp", "tensor"),
            P("dp", "tensor"),
            P("tensor", "dp"),
        ),
        check_vma=False,
    )
```
